32 devices in a mesh: band: 4 (over x, core), col: 8 (over z, y).
Axes of the slice: x: 2, y: 2, z: 4, core: 2. Of those that a mesh axis runs over, the one named last changes fastest.
Arguments:
- left_image: bfloat16 [16, 1024, 256], P('band', 'col'), may hold values from -6 to 6
- right_image: bfloat16 [16, 1024, 256], P('band', 'col'), may hold values from -6 to 6
- kernel: bfloat16 [2304, 256], replicated, may hold values from -0.125 to 0.125
- valid_mask: int32 [16, 1024], P('band', 'col'), may hold values 0 or 1
- disparity: int32 [16, 1024], P('band', 'col'), may hold values from 0 to 511
Outputs:
- grad_left: bfloat16 [16, 1024, 256], P('band', 'col')
- grad_right: bfloat16 [16, 1024, 256], P('band', 'col')
The draws below stay inside these ranges and needn't reach their ends.
All inputs are finite; a program needn't handle non-finite values. No bound on the sum of `valid_mask` on one device may be relied on, other than what follows from the above.
Results may differ from the reference program's by a relative error of at most 0.011.
Values may be sent and summed in bfloat16 or wider, within the bound.
A program may use at most 64 MiB of HBM per device.

```python
import jax
import jax.numpy as jnp
from jax import lax

C = 256
DISP = 512
COLS_DEV = 128
HEIGHT = 16
WIDTH = 1024


def plant(result, stream_key, smallest, top_value):
    longest = result.shape.index(max(result.shape))
    spots = []
    for shift in (0, 1):
        where = [jax.random.randint(jax.random.fold_in(stream_key, axis), (), 0, length) for axis, length in enumerate(result.shape)]
        where[longest] = (where[longest] + shift) % result.shape[longest]
        spots.append(tuple(where))
    return result.at[spots[0]].set(smallest).at[spots[1]].set(top_value)


def shard_levels(own_key, extent, shards, least, high):
    gain = 1.0
    for position, blocks in shards:
        steps = jax.random.uniform(jax.random.fold_in(jax.random.fold_in(own_key, 6), position), (blocks,), jnp.float32, least / len(shards), high / len(shards))
        gain = gain * jnp.repeat(jnp.exp(steps), extent[position] // blocks).reshape((-1,) + (1,) * (len(extent) - 1 - position))
    return gain


def bell_draw(key, extent, spread, reach, shards=(), kind=jnp.bfloat16):
    result = jax.random.normal(key, extent, jnp.float32) * spread
    if len(shards) > 0:
        result = shard_levels(key, extent, shards, -0.22, 0.18) * result
    return jnp.clip(result, min=-reach, max=reach).astype(kind)


def setup_inputs(seed: int = 0) -> dict:
    key_list = jax.random.split(jax.random.key(seed), 6)
    return {
        "left_image": bell_draw(key_list[0], (HEIGHT, WIDTH, C), 1.0, 6.0, ((0, 4), (1, 8))),
        "right_image": bell_draw(key_list[1], (HEIGHT, WIDTH, C), 1.0, 6.0, ((0, 4), (1, 8))),
        "kernel": bell_draw(key_list[2], (9 * C, C), (9 * C) ** -0.5, 0.125),
        "valid_mask": plant((jax.random.randint(key_list[3], (HEIGHT, WIDTH), 0, 4) < 3).astype(jnp.int32), jax.random.fold_in(key_list[3], 1), 0, 1),
        "disparity": plant(jax.random.randint(key_list[4], (HEIGHT, WIDTH), 0, DISP), jax.random.fold_in(key_list[4], 1), 0, DISP - 1).astype(jnp.int32),
    }


def conv_image(image_in, weights):
    height = image_in.shape[0]
    columns = image_in.shape[1]
    padded = jnp.pad(image_in, ((1, 1), (1, 1), (0, 0)))

    def one_row(row_index):
        window = lax.dynamic_slice_in_dim(padded, row_index, 3, 0)
        pieces = [window[row_off, col_off:col_off + columns] for row_off in range(3) for col_off in range(3)]
        patches = jnp.concatenate(pieces, axis=1)
        return jnp.dot(patches, weights, preferred_element_type=jnp.float32)

    return lax.map(one_row, jnp.arange(height, dtype=jnp.int32))


def flip_kernel(kernel):
    blocks = kernel.reshape(3, 3, C, C)[::-1, ::-1]
    return jnp.transpose(blocks, (0, 1, 3, 2)).reshape(9 * C, C)


def row_terms(left_row, right_row, mask_row, truth_row):
    columns = left_row.shape[0]
    right_pad = jnp.concatenate([jnp.zeros((DISP, C), right_row.dtype), right_row], 0)
    disparities = jnp.arange(DISP, dtype=jnp.int32)
    inner = jnp.arange(COLS_DEV, dtype=jnp.int32)
    lookup = inner[:, None] + DISP - disparities[None, :]
    factor = C ** -0.5

    def column_block(running, offset):
        left_block = lax.dynamic_slice_in_dim(left_row, offset, COLS_DEV, 0)
        segment = lax.dynamic_slice_in_dim(right_pad, offset, COLS_DEV + DISP, 0)
        scores = jnp.dot(left_block, segment.T, preferred_element_type=jnp.float32) * factor
        correlation = jnp.take_along_axis(scores, lookup, axis=1)
        validity = lax.dynamic_slice_in_dim(mask_row, offset, COLS_DEV, 0).astype(jnp.float32)
        truth_block = lax.dynamic_slice_in_dim(truth_row, offset, COLS_DEV, 0)
        distance = (disparities[None, :] - truth_block[:, None]).astype(jnp.float32)
        target = jnp.exp(-distance * distance / 8.0)
        gradient = (validity[:, None] * (correlation - target) * (C / DISP)).astype(jnp.bfloat16)
        banded = jnp.zeros((COLS_DEV, COLS_DEV + DISP), gradient.dtype).at[inner[:, None], lookup].set(gradient)
        left_term = jnp.dot(banded, segment, preferred_element_type=jnp.float32) * factor
        right_term = jnp.dot(banded.T, left_block, preferred_element_type=jnp.float32) * factor
        current = lax.dynamic_slice_in_dim(running, offset, COLS_DEV + DISP, 0)
        running = lax.dynamic_update_slice_in_dim(running, current + right_term, offset, 0)
        return running, left_term

    offsets = jnp.arange(0, columns, COLS_DEV, dtype=jnp.int32)
    initial = jnp.zeros((DISP + columns, C), jnp.float32)
    right_sum, left_parts = lax.scan(column_block, initial, offsets)
    return left_parts.reshape(columns, C), right_sum[DISP:]


def reference(left_image, right_image, kernel, valid_mask, disparity):
    left_feat = conv_image(left_image, kernel).astype(jnp.bfloat16)
    right_feat = conv_image(right_image, kernel).astype(jnp.bfloat16)

    def one_row(items):
        return row_terms(items[0], items[1], items[2], items[3])

    dleft, dright = lax.map(one_row, (left_feat, right_feat, valid_mask, disparity))
    flipped = flip_kernel(kernel)
    grad_left = conv_image(dleft.astype(jnp.bfloat16), flipped).astype(jnp.bfloat16)
    grad_right = conv_image(dright.astype(jnp.bfloat16), flipped).astype(jnp.bfloat16)
    return grad_left, grad_right
```

```python
import jax
import jax.numpy as jnp
from jax import lax
from jax.experimental import pallas as pl
from jax.experimental.pallas import tpu as pltpu
from jax.sharding import PartitionSpec as P

DISP = 512
EDGE = 16
MESH = pl.DeviceIdType.MESH
SIDES = [(-1, 0), (1, 0), (0, -1), (0, 1), (-1, -1), (-1, 1), (1, -1), (1, 1)]
NT = (((1,), (1,)), ((), ()))
TN = (((0,), (0,)), ((), ()))


def guarded(cond, action):
    if cond is True:
        action()
    else:
        pl.when(cond)(action)


def both(first, second):
    if first is True:
        return second
    if second is True:
        return first
    return jnp.logical_and(first, second)


def kernel(
    bands, cols, left_ref, right_ref, kernel_ref, valid_ref, truth_ref, gl_ref, gr_ref,
    image, weights, seg, lfeat, grad, terms, to_partner, to_far, to_near,
    from_partner, from_far, from_near,
    local_sem, halo_send, halo_recv, fwd_send, fwd_recv, rev_send, rev_recv,
):
    band = lax.axis_index("band")
    col = lax.axis_index("col")
    height, columns, channels = left_ref.shape
    reach = DISP // columns
    wide = columns + 2 * EDGE
    factor = channels ** (-0.5)
    even = lax.rem(col, 2) == 0
    odd = jnp.logical_not(even)
    partner = jnp.where(even, col + 1, col - 1)
    images = (left_ref, right_ref)
    pending = []

    def inside(step_b, step_c):
        cond = True
        if step_b < 0:
            cond = both(cond, band + step_b >= 0)
        if step_b > 0:
            cond = both(cond, band + step_b < bands)
        if step_c < 0:
            cond = both(cond, col + step_c >= 0)
        if step_c > 0:
            cond = both(cond, col + step_c < cols)
        return cond

    def send(cond, src, dst, sem_out, sem_in, to_band, to_col):
        def describe():
            return pltpu.make_async_remote_copy(
                src_ref=src, dst_ref=dst, send_sem=sem_out, recv_sem=sem_in,
                device_id={"band": to_band, "col": to_col}, device_id_type=MESH,
            )

        guarded(cond, lambda: describe().start())
        pending.append((cond, describe))

    def arrive(cond, dst, sem_out, sem_in):
        def wait():
            pltpu.make_async_remote_copy(
                src_ref=dst, dst_ref=dst, send_sem=sem_out, recv_sem=sem_in,
                device_id={"band": band, "col": partner}, device_id_type=MESH,
            ).wait_recv()

        guarded(cond, wait)

    def send_span(step, size, edge):
        return (0, edge) if step < 0 else ((size - edge, edge) if step > 0 else (0, size))

    def land_span(step, size, edge):
        return (size + edge, edge) if step < 0 else ((0, edge) if step > 0 else (edge, size))

    def halo_out(source, pad, which, picked=SIDES):
        for side in picked:
            number = SIDES.index(side)
            row, rows = send_span(side[0], height, 1)
            first, count = send_span(side[1], columns, EDGE)
            to_row, _ = land_span(side[0], height, 1)
            to_first, _ = land_span(side[1], columns, EDGE)
            send(
                inside(*side),
                source(row, rows, first, count),
                pad.at[which % 2, pl.ds(to_row, rows), pl.ds(to_first, count)],
                halo_send.at[which, number], halo_recv.at[which, number],
                band + side[0], col + side[1],
            )

    def halo_in(pad, which):
        for number, side in enumerate(SIDES):
            to_row, rows = land_span(side[0], height, 1)
            to_first, count = land_span(side[1], columns, EDGE)
            arrive(
                inside(-side[0], -side[1]),
                pad.at[which % 2, pl.ds(to_row, rows), pl.ds(to_first, count)],
                halo_send.at[which, number], halo_recv.at[which, number],
            )

    def convolve(pad, which, backward):
        rows = [
            pad[which, pl.ds(a, height)].reshape(height * wide, channels) for a in range(3)
        ]
        total = None
        for b in range(3):
            acc = None
            for a in range(3):
                block = weights[pl.ds((3 * a + b) * channels, channels), :]
                if backward:
                    part = lax.dot_general(
                        rows[2 - a], block, NT, preferred_element_type=jnp.float32
                    )
                else:
                    part = jnp.dot(rows[a], block, preferred_element_type=jnp.float32)
                acc = part if acc is None else acc + part
            shift = (b - 1) if backward else (1 - b)
            if shift != 0:
                acc = pltpu.roll(acc, shift % (height * wide), 0)
            total = acc if total is None else total + acc
        total = total.reshape(height, wide, channels)[:, EDGE : EDGE + columns]
        return total.astype(jnp.bfloat16)

    core = (pl.ds(1, height), pl.ds(EDGE, columns))
    locals_in = [
        pltpu.make_async_copy(right_ref, image.at[(1,) + core], local_sem.at[0]),
        pltpu.make_async_copy(left_ref, image.at[(0,) + core], local_sem.at[1]),
        pltpu.make_async_copy(kernel_ref, weights, local_sem.at[2]),
    ]
    for copy in locals_in:
        copy.start()

    for pad in (image, grad):
        for which in range(2):
            for row in (0, height + 1):
                pad[which, row] = jnp.zeros((wide, channels), jnp.bfloat16)
            for first in (0, EDGE + columns):
                pad[which, 1 : height + 1, first : first + EDGE] = jnp.zeros(
                    (height, EDGE, channels), jnp.bfloat16
                )
    for k in range(1, reach + 1):
        @pl.when(col < k)
        def _(k=k):
            seg[:, k] = jnp.zeros((height, columns, channels), jnp.bfloat16)

    barrier = pltpu.get_barrier_semaphore()
    met = jnp.int32(0)
    for side in SIDES + [(0, -2), (0, 2)]:
        cond = inside(*side)

        def greet(side=side):
            pl.semaphore_signal(
                barrier, inc=1,
                device_id={"band": band + side[0], "col": col + side[1]}, device_id_type=MESH,
            )

        guarded(cond, greet)
        met = met + cond.astype(jnp.int32)
    pl.semaphore_wait(barrier, met)

    for which in (1, 0):
        halo_out(
            lambda row, rows, first, count: images[which].at[pl.ds(row, rows), pl.ds(first, count)],
            image, which,
        )
    locals_in[0].wait()
    locals_in[2].wait()
    halo_in(image, 1)
    seg[:, 0] = convolve(image, 1, False)

    two_down, four_down = col >= 2, col >= 4
    two_up = col + 2 < cols
    for r in range(height):
        send(two_up, seg.at[r, 0], seg.at[r, 2], fwd_send.at[0, r], fwd_recv.at[2, r], band, col + 2)
        send(even, seg.at[r, 0], seg.at[r, 1], fwd_send.at[1, r], fwd_recv.at[1, r], band, partner)

    locals_in[1].wait()
    halo_in(image, 0)
    lfeat[...] = convolve(image, 0, False)

    down = lax.broadcasted_iota(jnp.int32, (reach + 1, columns, columns), 1)
    across = lax.broadcasted_iota(jnp.int32, (reach + 1, columns, columns), 2)
    order = lax.broadcasted_iota(jnp.int32, (reach + 1, columns, columns), 0)
    offset = order * columns + across - down
    tall = (reach + 1) * columns

    def pass_near(r):
        arrive(two_down, seg.at[r, 2], fwd_send.at[0, r], fwd_recv.at[2, r])
        send(both(two_down, two_up), seg.at[r, 2], seg.at[r, 4],
             fwd_send.at[2, r], fwd_recv.at[4, r], band, col + 2)
        send(both(two_down, even), seg.at[r, 2], seg.at[r, 3],
             fwd_send.at[3, r], fwd_recv.at[3, r], band, partner)
        send(both(two_down, odd), seg.at[r, 2], seg.at[r, 1],
             fwd_send.at[3, r], fwd_recv.at[1, r], band, partner)

    def pass_far(r):
        arrive(four_down, seg.at[r, 4], fwd_send.at[2, r], fwd_recv.at[4, r])
        send(both(four_down, odd), seg.at[r, 4], seg.at[r, 3],
             fwd_send.at[1, r], fwd_recv.at[3, r], band, partner)

    def correlate(r):
        arrive(jnp.logical_or(odd, two_down), seg.at[r, 1], fwd_send.at[1, r], fwd_recv.at[1, r])
        arrive(jnp.logical_or(both(odd, two_down), four_down), seg.at[r, 3],
               fwd_send.at[3, r], fwd_recv.at[3, r])
        block = seg[r].reshape(tall, channels)
        left = lfeat[r]
        scores = lax.dot_general(block, left, NT, preferred_element_type=jnp.float32) * factor
        scores = scores.reshape(reach + 1, columns, columns)
        distance = (offset - truth_ref[r : r + 1, :].reshape(1, 1, columns)).astype(jnp.float32)
        target = jnp.exp(distance * distance * (-1.0 / 8.0))
        scale = valid_ref[r : r + 1, :].astype(jnp.float32).reshape(1, 1, columns) * (channels / DISP)
        slope = scale * (scores - target)
        slope = jnp.where(jnp.logical_and(offset >= 0, offset < DISP), slope, 0.0)
        slope = slope.astype(jnp.bfloat16).reshape(tall, columns)
        term = jnp.dot(slope, left, preferred_element_type=jnp.float32) * factor
        terms[r] = term.reshape(reach + 1, columns, channels)
        to_partner[r, 0] = terms[r, 1].astype(jnp.bfloat16)
        to_partner[r, 1] = terms[r, 3].astype(jnp.bfloat16)
        send(jnp.logical_or(odd, two_down), to_partner.at[r, 0], from_partner.at[r, 0],
             rev_send.at[0, r], rev_recv.at[0, r], band, partner)
        send(jnp.logical_or(both(odd, two_down), four_down), to_partner.at[r, 1],
             from_partner.at[r, 1], rev_send.at[1, r], rev_recv.at[1, r], band, partner)
        dleft = lax.dot_general(slope, block, TN, preferred_element_type=jnp.float32) * factor
        grad[0, r + 1, pl.ds(EDGE, columns)] = dleft.astype(jnp.bfloat16)

    def add_partner(r, place, k):
        terms[r, k] = terms[r, k] + from_partner[r, place].astype(jnp.float32)

    def return_far(r):
        arrive(jnp.logical_or(even, two_down), from_partner.at[r, 0],
               rev_send.at[0, r], rev_recv.at[0, r])
        arrive(jnp.logical_or(both(even, two_down), four_down), from_partner.at[r, 1],
               rev_send.at[1, r], rev_recv.at[1, r])
        pl.when(both(odd, four_down))(lambda: add_partner(r, 1, 4))
        to_far[r] = terms[r, 4].astype(jnp.bfloat16)
        send(four_down, to_far.at[r], from_far.at[r],
             rev_send.at[2, r], rev_recv.at[2, r], band, col - 2)
        pl.when(both(odd, two_down))(lambda: add_partner(r, 0, 2))
        pl.when(both(even, two_down))(lambda: add_partner(r, 1, 2))
        pl.when(even)(lambda: add_partner(r, 0, 0))

    def return_near(r):
        @pl.when(both(two_down, two_up))
        def _():
            arrive(True, from_far.at[r], rev_send.at[2, r], rev_recv.at[2, r])
            terms[r, 2] = terms[r, 2] + from_far[r].astype(jnp.float32)

        to_near[r] = terms[r, 2].astype(jnp.bfloat16)
        send(two_down, to_near.at[r], from_near.at[r],
             rev_send.at[3, r], rev_recv.at[3, r], band, col - 2)

    def settle(r):
        @pl.when(two_up)
        def _():
            arrive(True, from_near.at[r], rev_send.at[3, r], rev_recv.at[3, r])
            terms[r, 0] = terms[r, 0] + from_near[r].astype(jnp.float32)

        grad[1, r + 1, pl.ds(EDGE, columns)] = terms[r, 0].astype(jnp.bfloat16)

    stages = ((pass_near, 0), (pass_far, 1), (correlate, 1), (return_far, 2), (return_near, 3))
    for step in range(height + 3):
        for stage, lag in stages:
            if 0 <= step - lag < height:
                stage(step - lag)
        if step == height:
            halo_out(
                lambda row, rows, first, count: grad.at[0, pl.ds(1 + row, rows), pl.ds(EDGE + first, count)],
                grad, 2,
            )
    halo_in(grad, 2)
    gl_ref[...] = convolve(grad, 0, True)
    for r in range(height):
        settle(r)
    halo_out(
        lambda row, rows, first, count: grad.at[1, pl.ds(1 + row, rows), pl.ds(EDGE + first, count)],
        grad, 3,
    )
    halo_in(grad, 3)
    gr_ref[...] = convolve(grad, 1, True)
    for cond, describe in pending:
        guarded(cond, lambda: describe().wait_send())


def solution(mesh):
    bands, cols = mesh.shape["band"], mesh.shape["col"]

    def shards(left_image, right_image, weights, valid_mask, disparity):
        height, columns, channels = left_image.shape
        reach = DISP // columns
        wide = columns + 2 * EDGE
        bf16 = jnp.bfloat16
        any_spec = pl.BlockSpec(memory_space=pl.ANY)
        vmem_spec = pl.BlockSpec(memory_space=pltpu.VMEM)
        dma = pltpu.SemaphoreType.DMA
        pad = pltpu.VMEM((2, height + 2, wide, channels), bf16)
        rows = pltpu.VMEM((height, columns, channels), bf16)
        pairs = pltpu.VMEM((height, 2, columns, channels), bf16)

        def body(*refs):
            kernel(bands, cols, *refs)

        return pl.pallas_call(
            body,
            out_shape=(
                jax.ShapeDtypeStruct(left_image.shape, bf16),
                jax.ShapeDtypeStruct(right_image.shape, bf16),
            ),
            in_specs=[any_spec, any_spec, any_spec, vmem_spec, vmem_spec],
            out_specs=(vmem_spec, vmem_spec),
            scratch_shapes=[
                pad,
                pltpu.VMEM(weights.shape, bf16),
                pltpu.VMEM((height, reach + 1, columns, channels), bf16),
                rows,
                pad,
                pltpu.VMEM((height, reach + 1, columns, channels), jnp.float32),
                pairs, rows, rows,
                pairs, rows, rows,
                dma((3,)),
                dma((4, 8)), dma((4, 8)),
                dma((4, height)), dma((reach + 1, height)),
                dma((4, height)), dma((4, height)),
            ],
            compiler_params=pltpu.CompilerParams(
                collective_id=0, has_side_effects=True, vmem_limit_bytes=48 * 2**20
            ),
            cost_estimate=pl.CostEstimate(
                flops=5_000_000_000, bytes_accessed=4_000_000, transcendentals=400_000
            ),
        )(left_image, right_image, weights, valid_mask, disparity)

    return jax.shard_map(
        shards,
        mesh=mesh,
        in_specs=(
            P("band", "col", None),
            P("band", "col", None),
            P(),
            P("band", "col"),
            P("band", "col"),
        ),
        out_specs=(P("band", "col", None), P("band", "col", None)),
        check_vma=False,
    )
```

```python
import jax
import jax.numpy as jnp
from jax import lax
from jax.experimental import pallas as pl
from jax.experimental.pallas import tpu as pltpu
from jax.sharding import PartitionSpec as P

DISP = 512
EDGE = 16
MESH = pl.DeviceIdType.MESH
SIDES = [(-1, 0), (1, 0), (0, -1), (0, 1), (-1, -1), (-1, 1), (1, -1), (1, 1)]
NT = (((1,), (1,)), ((), ()))
TN = (((0,), (0,)), ((), ()))


def guarded(cond, action):
    if cond is True:
        action()
    else:
        pl.when(cond)(action)


def both(first, second):
    if first is True:
        return second
    if second is True:
        return first
    return jnp.logical_and(first, second)


def kernel(
    bands, cols, left_ref, right_ref, kernel_ref, valid_ref, truth_ref, gl_ref, gr_ref,
    image, weights, truth, valid, seg, lfeat, left_sum, grad, terms, results,
    to_partner, to_far, to_near, from_partner, from_far, from_near,
    local_sem, halo_send, halo_recv, fwd_send, fwd_recv, rev_send, rev_recv,
    left_send, left_recv, side_send, side_recv,
):
    band = lax.axis_index("band")
    col = lax.axis_index("col")
    height, columns, channels = left_ref.shape
    slots = DISP // columns // 2 + 1
    wide = columns + 2 * EDGE
    factor = channels ** (-0.5)
    even = lax.rem(col, 2) == 0
    odd = jnp.logical_not(even)
    partner = jnp.where(even, col + 1, col - 1)
    images = (left_ref, right_ref)
    pending = []

    def inside(step_b, step_c):
        cond = True
        if step_b < 0:
            cond = both(cond, band + step_b >= 0)
        if step_b > 0:
            cond = both(cond, band + step_b < bands)
        if step_c < 0:
            cond = both(cond, col + step_c >= 0)
        if step_c > 0:
            cond = both(cond, col + step_c < cols)
        return cond

    def send(cond, src, dst, sem_out, sem_in, to_band, to_col):
        def describe():
            return pltpu.make_async_remote_copy(
                src_ref=src, dst_ref=dst, send_sem=sem_out, recv_sem=sem_in,
                device_id={"band": to_band, "col": to_col}, device_id_type=MESH,
            )

        guarded(cond, lambda: describe().start())
        pending.append((cond, describe))

    def arrive(cond, dst, sem_out, sem_in):
        def wait():
            pltpu.make_async_remote_copy(
                src_ref=dst, dst_ref=dst, send_sem=sem_out, recv_sem=sem_in,
                device_id={"band": band, "col": partner}, device_id_type=MESH,
            ).wait_recv()

        guarded(cond, wait)

    def send_span(step, size, edge):
        return (0, edge) if step < 0 else ((size - edge, edge) if step > 0 else (0, size))

    def land_span(step, size, edge):
        return (size + edge, edge) if step < 0 else ((0, edge) if step > 0 else (edge, size))

    def halo_out(source, pad, which, picked=SIDES):
        for side in picked:
            number = SIDES.index(side)
            row, rows = send_span(side[0], height, 1)
            first, count = send_span(side[1], columns, EDGE)
            to_row, _ = land_span(side[0], height, 1)
            to_first, _ = land_span(side[1], columns, EDGE)
            send(
                inside(*side),
                source(row, rows, first, count),
                pad.at[which % 2, pl.ds(to_row, rows), pl.ds(to_first, count)],
                halo_send.at[which, number], halo_recv.at[which, number],
                band + side[0], col + side[1],
            )

    def halo_in(pad, which):
        for number, side in enumerate(SIDES):
            to_row, rows = land_span(side[0], height, 1)
            to_first, count = land_span(side[1], columns, EDGE)
            arrive(
                inside(-side[0], -side[1]),
                pad.at[which % 2, pl.ds(to_row, rows), pl.ds(to_first, count)],
                halo_send.at[which, number], halo_recv.at[which, number],
            )

    def convolve(pad, which, backward):
        rows = [
            pad[which, pl.ds(a, height)].reshape(height * wide, channels) for a in range(3)
        ]
        total = None
        for b in range(3):
            acc = None
            for a in range(3):
                block = weights[pl.ds((3 * a + b) * channels, channels), :]
                if backward:
                    part = lax.dot_general(
                        rows[2 - a], block, NT, preferred_element_type=jnp.float32
                    )
                else:
                    part = jnp.dot(rows[a], block, preferred_element_type=jnp.float32)
                acc = part if acc is None else acc + part
            shift = (b - 1) if backward else (1 - b)
            if shift != 0:
                acc = pltpu.roll(acc, shift % (height * wide), 0)
            total = acc if total is None else total + acc
        total = total.reshape(height, wide, channels)[:, EDGE : EDGE + columns]
        return total.astype(jnp.bfloat16)

    core = (pl.ds(1, height), pl.ds(EDGE, columns))
    locals_in = [
        pltpu.make_async_copy(right_ref, image.at[(1,) + core], local_sem.at[0]),
        pltpu.make_async_copy(left_ref, image.at[(0,) + core], local_sem.at[1]),
        pltpu.make_async_copy(kernel_ref, weights, local_sem.at[2]),
        pltpu.make_async_copy(truth_ref, truth.at[0], local_sem.at[3]),
        pltpu.make_async_copy(valid_ref, valid.at[0], local_sem.at[4]),
    ]
    for copy in locals_in:
        copy.start()

    for pad in (image, grad):
        for which in range(2):
            for row in (0, height + 1):
                pad[which, row] = jnp.zeros((wide, channels), jnp.bfloat16)
            for first in (0, EDGE + columns):
                pad[which, 1 : height + 1, first : first + EDGE] = jnp.zeros(
                    (height, EDGE, channels), jnp.bfloat16
                )
    for k in range(1, slots):
        @pl.when(col < 2 * k)
        def _(k=k):
            seg[:, k] = jnp.zeros((height, columns, channels), jnp.bfloat16)

    barrier = pltpu.get_barrier_semaphore()
    met = jnp.int32(0)
    for side in SIDES + [(0, -2), (0, 2)]:
        cond = inside(*side)

        def greet(side=side):
            pl.semaphore_signal(
                barrier, inc=1,
                device_id={"band": band + side[0], "col": col + side[1]}, device_id_type=MESH,
            )

        guarded(cond, greet)
        met = met + cond.astype(jnp.int32)
    pl.semaphore_wait(barrier, met)

    for which in (1, 0):
        halo_out(
            lambda row, rows, first, count: images[which].at[pl.ds(row, rows), pl.ds(first, count)],
            image, which,
        )
    send(True, truth_ref, truth.at[1], side_send.at[0], side_recv.at[0], band, partner)
    send(True, valid_ref, valid.at[1], side_send.at[1], side_recv.at[1], band, partner)
    locals_in[0].wait()
    locals_in[2].wait()
    halo_in(image, 1)
    seg[:, 0] = convolve(image, 1, False)

    two_down, four_down = col >= 2, col >= 4
    two_up = col + 2 < cols

    def own_up(r):
        send(two_up, seg.at[r, 0], seg.at[r, 1], fwd_send.at[0, r], fwd_recv.at[0, r], band, col + 2)

    own_up(0)
    own_up(1)
    locals_in[1].wait()
    halo_in(image, 0)
    lfeat[0] = convolve(image, 0, False)
    for r in range(height):
        send(True, lfeat.at[0, r], lfeat.at[1, r], left_send.at[0, r], left_recv.at[0, r], band, partner)
    for copy in locals_in[3:]:
        copy.wait()
    arrive(True, truth.at[1], side_send.at[0], side_recv.at[0])
    arrive(True, valid.at[1], side_send.at[1], side_recv.at[1])

    odd_slot = odd.astype(jnp.int32)

    def pass_near(r):
        arrive(two_down, seg.at[r, 1], fwd_send.at[0, r], fwd_recv.at[0, r])
        send(both(two_down, two_up), seg.at[r, 1], seg.at[r, 2],
             fwd_send.at[1, r], fwd_recv.at[1, r], band, col + 2)
        if r + 2 < height:
            own_up(r + 2)

    def slopes(r, who, block, first, count):
        shape = (count, columns, columns)
        offset = (
            (2 * lax.broadcasted_iota(jnp.int32, shape, 0) + first) * columns
            + lax.broadcasted_iota(jnp.int32, shape, 2)
            - lax.broadcasted_iota(jnp.int32, shape, 1)
        )
        left = lfeat[who, r]
        scores = lax.dot_general(block, left, NT, preferred_element_type=jnp.float32) * factor
        scores = scores.reshape(shape)
        distance = (offset - truth[who, r : r + 1, :].reshape(1, 1, columns)).astype(jnp.float32)
        target = jnp.exp(distance * distance * (-1.0 / 8.0))
        scale = valid[who, r : r + 1, :].astype(jnp.float32).reshape(1, 1, columns)
        slope = scale * (scores - target) * (channels / DISP)
        slope = jnp.where(jnp.logical_and(offset >= 0, offset < DISP), slope, 0.0)
        slope = slope.astype(jnp.bfloat16).reshape(count * columns, columns)
        term = jnp.dot(slope, left, preferred_element_type=jnp.float32) * factor
        dleft = lax.dot_general(slope, block, TN, preferred_element_type=jnp.float32) * factor
        return term.reshape(count, columns, channels), dleft

    def correlate(r):
        arrive(four_down, seg.at[r, 2], fwd_send.at[1, r], fwd_recv.at[1, r])
        arrive(True, lfeat.at[1, r], left_send.at[0, r], left_recv.at[0, r])
        block = seg[r, pl.ds(odd_slot, slots - 1)].reshape((slots - 1) * columns, channels)
        other, other_left = slopes(r, 1, block, 1, slots - 1)
        to_partner[r] = other_left.astype(jnp.bfloat16)
        send(True, to_partner.at[r], from_partner.at[r],
             left_send.at[1, r], left_recv.at[1, r], band, partner)
        own, own_left = slopes(r, 0, seg[r].reshape(slots * columns, channels), 0, slots)
        terms[r] = own
        terms[r, pl.ds(odd_slot, slots - 1)] = terms[r, pl.ds(odd_slot, slots - 1)] + other
        to_far[r] = terms[r, 2].astype(jnp.bfloat16)
        send(four_down, to_far.at[r], from_far.at[r],
             rev_send.at[0, r], rev_recv.at[0, r], band, col - 2)
        left_sum[r] = own_left

    def return_near(r):
        @pl.when(both(two_down, two_up))
        def _():
            arrive(True, from_far.at[r], rev_send.at[0, r], rev_recv.at[0, r])
            terms[r, 1] = terms[r, 1] + from_far[r].astype(jnp.float32)

        to_near[r] = terms[r, 1].astype(jnp.bfloat16)
        send(two_down, to_near.at[r], from_near.at[r],
             rev_send.at[1, r], rev_recv.at[1, r], band, col - 2)

    def settle_left(r):
        arrive(True, from_partner.at[r], left_send.at[1, r], left_recv.at[1, r])
        total = left_sum[r] + from_partner[r].astype(jnp.float32)
        grad[0, r + 1, pl.ds(EDGE, columns)] = total.astype(jnp.bfloat16)

    def settle(r):
        @pl.when(two_up)
        def _():
            arrive(True, from_near.at[r], rev_send.at[1, r], rev_recv.at[1, r])
            terms[r, 0] = terms[r, 0] + from_near[r].astype(jnp.float32)

        grad[1, r + 1, pl.ds(EDGE, columns)] = terms[r, 0].astype(jnp.bfloat16)

    def grads_out(which):
        halo_out(
            lambda row, rows, first, count: grad.at[which, pl.ds(1 + row, rows), pl.ds(EDGE + first, count)],
            grad, 2 + which,
        )

    stages = ((pass_near, 0), (correlate, 1), (return_near, 2))
    for step in range(height + 2):
        for stage, lag in stages:
            if 0 <= step - lag < height:
                stage(step - lag)
    for r in range(height):
        settle_left(r)
    grads_out(0)
    for r in range(height):
        settle(r)
    grads_out(1)
    halo_in(grad, 2)
    results[0] = convolve(grad, 0, True)
    out_left = pltpu.make_async_copy(results.at[0], gl_ref, local_sem.at[5])
    out_left.start()
    halo_in(grad, 3)
    results[1] = convolve(grad, 1, True)
    out_right = pltpu.make_async_copy(results.at[1], gr_ref, local_sem.at[6])
    out_right.start()
    for cond, describe in pending:
        guarded(cond, lambda: describe().wait_send())
    out_left.wait()
    out_right.wait()


def solution(mesh):
    bands, cols = mesh.shape["band"], mesh.shape["col"]

    def shards(left_image, right_image, weights, valid_mask, disparity):
        height, columns, channels = left_image.shape
        slots = DISP // columns // 2 + 1
        wide = columns + 2 * EDGE
        bf16 = jnp.bfloat16
        any_spec = pl.BlockSpec(memory_space=pl.ANY)
        dma = pltpu.SemaphoreType.DMA
        pad = pltpu.VMEM((2, height + 2, wide, channels), bf16)
        rows = pltpu.VMEM((height, columns, channels), bf16)
        both_rows = pltpu.VMEM((2, height, columns, channels), bf16)
        pixels = pltpu.VMEM((2, height, columns), jnp.int32)

        def body(*refs):
            kernel(bands, cols, *refs)

        return pl.pallas_call(
            body,
            out_shape=(
                jax.ShapeDtypeStruct(left_image.shape, bf16),
                jax.ShapeDtypeStruct(right_image.shape, bf16),
            ),
            in_specs=[any_spec] * 5,
            out_specs=(any_spec, any_spec),
            scratch_shapes=[
                pad,
                pltpu.VMEM(weights.shape, bf16),
                pixels, pixels,
                pltpu.VMEM((height, slots, columns, channels), bf16),
                both_rows,
                pltpu.VMEM((height, columns, channels), jnp.float32),
                pad,
                pltpu.VMEM((height, slots, columns, channels), jnp.float32),
                both_rows,
                rows, rows, rows,
                rows, rows, rows,
                dma((7,)),
                dma((4, 8)), dma((4, 8)),
                dma((2, height)), dma((2, height)),
                dma((2, height)), dma((2, height)),
                dma((2, height)), dma((2, height)),
                dma((2,)), dma((2,)),
            ],
            compiler_params=pltpu.CompilerParams(
                collective_id=0, has_side_effects=True, vmem_limit_bytes=60 * 2**20
            ),
            cost_estimate=pl.CostEstimate(
                flops=5_000_000_000, bytes_accessed=4_000_000, transcendentals=400_000
            ),
        )(left_image, right_image, weights, valid_mask, disparity)

    return jax.shard_map(
        shards,
        mesh=mesh,
        in_specs=(
            P("band", "col", None),
            P("band", "col", None),
            P(),
            P("band", "col"),
            P("band", "col"),
        ),
        out_specs=(P("band", "col", None), P("band", "col", None)),
        check_vma=False,
    )
```

```python
import jax
import jax.numpy as jnp
from jax import lax
from jax.experimental import pallas as pl
from jax.experimental.pallas import tpu as pltpu
from jax.sharding import PartitionSpec as P

DISP = 512
EDGE = 16
MESH = pl.DeviceIdType.MESH
SIDES = [(-1, 0), (1, 0), (0, -1), (0, 1), (-1, -1), (-1, 1), (1, -1), (1, 1)]
NT = (((1,), (1,)), ((), ()))
TN = (((0,), (0,)), ((), ()))


def guarded(cond, action):
    if cond is True:
        action()
    else:
        pl.when(cond)(action)


def both(first, second):
    if first is True:
        return second
    if second is True:
        return first
    return jnp.logical_and(first, second)


def kernel(
    bands, cols, left_ref, right_ref, kernel_ref, valid_ref, truth_ref, gl_ref, gr_ref,
    image, weights, flipped, truth, valid, seg, lfeat, left_sum, grad, terms, results,
    to_partner, to_far, to_near, from_partner, from_far, from_near,
    local_sem, halo_send, halo_recv, fwd_send, fwd_recv, rev_send, rev_recv,
    left_send, left_recv, side_send, side_recv,
):
    band = lax.axis_index("band")
    col = lax.axis_index("col")
    height, columns, channels = left_ref.shape
    slots = DISP // columns // 2 + 1
    wide = columns + 2 * EDGE
    factor = channels ** (-0.5)
    even = lax.rem(col, 2) == 0
    odd = jnp.logical_not(even)
    partner = jnp.where(even, col + 1, col - 1)
    images = (left_ref, right_ref)
    pending = []

    def inside(step_b, step_c):
        cond = True
        if step_b < 0:
            cond = both(cond, band + step_b >= 0)
        if step_b > 0:
            cond = both(cond, band + step_b < bands)
        if step_c < 0:
            cond = both(cond, col + step_c >= 0)
        if step_c > 0:
            cond = both(cond, col + step_c < cols)
        return cond

    def send(cond, src, dst, sem_out, sem_in, to_band, to_col):
        def describe():
            return pltpu.make_async_remote_copy(
                src_ref=src, dst_ref=dst, send_sem=sem_out, recv_sem=sem_in,
                device_id={"band": to_band, "col": to_col}, device_id_type=MESH,
            )

        guarded(cond, lambda: describe().start())
        pending.append((cond, describe))

    def arrive(cond, dst, sem_out, sem_in):
        def wait():
            pltpu.make_async_remote_copy(
                src_ref=dst, dst_ref=dst, send_sem=sem_out, recv_sem=sem_in,
                device_id={"band": band, "col": partner}, device_id_type=MESH,
            ).wait_recv()

        guarded(cond, wait)

    def send_span(step, size, edge):
        return (0, edge) if step < 0 else ((size - edge, edge) if step > 0 else (0, size))

    def land_span(step, size, edge):
        return (size + edge, edge) if step < 0 else ((0, edge) if step > 0 else (edge, size))

    def halo_out(source, pad, which, picked=SIDES):
        for side in picked:
            number = SIDES.index(side)
            row, rows = send_span(side[0], height, 1)
            first, count = send_span(side[1], columns, EDGE)
            to_row, _ = land_span(side[0], height, 1)
            to_first, _ = land_span(side[1], columns, EDGE)
            send(
                inside(*side),
                source(row, rows, first, count),
                pad.at[which % 2, pl.ds(to_row, rows), pl.ds(to_first, count)],
                halo_send.at[which, number], halo_recv.at[which, number],
                band + side[0], col + side[1],
            )

    def halo_in(pad, which):
        for number, side in enumerate(SIDES):
            to_row, rows = land_span(side[0], height, 1)
            to_first, count = land_span(side[1], columns, EDGE)
            arrive(
                inside(-side[0], -side[1]),
                pad.at[which % 2, pl.ds(to_row, rows), pl.ds(to_first, count)],
                halo_send.at[which, number], halo_recv.at[which, number],
            )

    def convolve(pad, which, backward):
        spans = ((0, EDGE + columns), (EDGE, columns), (EDGE, columns + EDGE))
        total = None
        for b in (1, 0, 2):
            side = 2 - b if backward else b
            first, count = spans[side]
            lines = jnp.concatenate(
                [
                    pad[which, pl.ds(2 - a if backward else a, height), pl.ds(first, count)]
                    .reshape(height * count, channels)
                    for a in range(3)
                ],
                1,
            )
            source = flipped if backward else weights
            blocks = jnp.concatenate(
                [source[pl.ds((3 * a + b) * channels, channels), :] for a in range(3)], 0
            )
            part = jnp.dot(lines, blocks, preferred_element_type=jnp.float32)
            if side != 1:
                part = pltpu.roll(part, (1 - side) % (height * count), 0)
            part = part.reshape(height, count, channels)
            part = part[:, EDGE:] if side == 0 else part[:, :columns]
            total = part if total is None else total + part
        return total

    core = (pl.ds(1, height), pl.ds(EDGE, columns))
    locals_in = [
        pltpu.make_async_copy(right_ref, image.at[(1,) + core], local_sem.at[0]),
        pltpu.make_async_copy(left_ref, image.at[(0,) + core], local_sem.at[1]),
        pltpu.make_async_copy(kernel_ref, weights, local_sem.at[2]),
        pltpu.make_async_copy(truth_ref, truth.at[0], local_sem.at[3]),
        pltpu.make_async_copy(valid_ref, valid.at[0], local_sem.at[4]),
    ]
    for copy in locals_in:
        copy.start()

    for pad in (image, grad):
        for which in range(2):
            for row in (0, height + 1):
                pad[which, row] = jnp.zeros((wide, channels), jnp.bfloat16)
            for first in (0, EDGE + columns):
                pad[which, 1 : height + 1, first : first + EDGE] = jnp.zeros(
                    (height, EDGE, channels), jnp.bfloat16
                )
    for k in range(1, slots):
        @pl.when(col < 2 * k)
        def _(k=k):
            seg[:, k] = jnp.zeros((height, columns, channels), jnp.bfloat16)

    barrier = pltpu.get_barrier_semaphore()
    met = jnp.int32(0)
    for side in SIDES + [(0, -2), (0, 2)]:
        cond = inside(*side)

        def greet(side=side):
            pl.semaphore_signal(
                barrier, inc=1,
                device_id={"band": band + side[0], "col": col + side[1]}, device_id_type=MESH,
            )

        guarded(cond, greet)
        met = met + cond.astype(jnp.int32)
    pl.semaphore_wait(barrier, met)

    for which in (1, 0):
        halo_out(
            lambda row, rows, first, count: images[which].at[pl.ds(row, rows), pl.ds(first, count)],
            image, which,
        )
    send(True, truth_ref, truth.at[1], side_send.at[0], side_recv.at[0], band, partner)
    send(True, valid_ref, valid.at[1], side_send.at[1], side_recv.at[1], band, partner)
    locals_in[0].wait()
    locals_in[2].wait()
    for position in range(9):
        place = pl.ds(position * channels, channels)
        flipped[place, :] = weights[place, :].T
    halo_in(image, 1)
    seg[:, 0] = convolve(image, 1, False).astype(jnp.bfloat16)

    two_down, four_down = col >= 2, col >= 4
    two_up = col + 2 < cols

    def own_up(r):
        send(two_up, seg.at[r, 0], seg.at[r, 1], fwd_send.at[0, r], fwd_recv.at[0, r], band, col + 2)

    own_up(0)
    own_up(1)
    locals_in[1].wait()
    halo_in(image, 0)
    lfeat[0] = convolve(image, 0, False).astype(jnp.bfloat16)
    for r in range(height):
        send(True, lfeat.at[0, r], lfeat.at[1, r], left_send.at[0, r], left_recv.at[0, r], band, partner)
    for copy in locals_in[3:]:
        copy.wait()
    arrive(True, truth.at[1], side_send.at[0], side_recv.at[0])
    arrive(True, valid.at[1], side_send.at[1], side_recv.at[1])

    odd_slot = odd.astype(jnp.int32)

    def pass_near(r):
        arrive(two_down, seg.at[r, 1], fwd_send.at[0, r], fwd_recv.at[0, r])
        send(both(two_down, two_up), seg.at[r, 1], seg.at[r, 2],
             fwd_send.at[1, r], fwd_recv.at[1, r], band, col + 2)
        if r + 2 < height:
            own_up(r + 2)

    def slopes(r, who, block, first, count):
        shape = (count, columns, columns)
        offset = (
            (2 * lax.broadcasted_iota(jnp.int32, shape, 0) + first) * columns
            + lax.broadcasted_iota(jnp.int32, shape, 2)
            - lax.broadcasted_iota(jnp.int32, shape, 1)
        )
        left = lfeat[who, r]
        scores = lax.dot_general(block, left, NT, preferred_element_type=jnp.float32) * factor
        scores = scores.reshape(shape)
        distance = (offset - truth[who, r : r + 1, :].reshape(1, 1, columns)).astype(jnp.float32)
        target = jnp.exp(distance * distance * (-1.0 / 8.0))
        scale = valid[who, r : r + 1, :].astype(jnp.float32).reshape(1, 1, columns)
        slope = scale * (scores - target) * (channels / DISP)
        slope = jnp.where(jnp.logical_and(offset >= 0, offset < DISP), slope, 0.0)
        slope = slope.astype(jnp.bfloat16).reshape(count * columns, columns)
        term = jnp.dot(slope, left, preferred_element_type=jnp.float32) * factor
        dleft = lax.dot_general(slope, block, TN, preferred_element_type=jnp.float32) * factor
        return term.reshape(count, columns, channels), dleft

    def correlate(r):
        arrive(four_down, seg.at[r, 2], fwd_send.at[1, r], fwd_recv.at[1, r])
        arrive(True, lfeat.at[1, r], left_send.at[0, r], left_recv.at[0, r])
        block = seg[r, pl.ds(odd_slot, slots - 1)].reshape((slots - 1) * columns, channels)
        other, other_left = slopes(r, 1, block, 1, slots - 1)
        to_partner[r] = other_left.astype(jnp.bfloat16)
        send(True, to_partner.at[r], from_partner.at[r],
             left_send.at[1, r], left_recv.at[1, r], band, partner)
        own, own_left = slopes(r, 0, seg[r].reshape(slots * columns, channels), 0, slots)
        terms[r] = own
        terms[r, pl.ds(odd_slot, slots - 1)] = terms[r, pl.ds(odd_slot, slots - 1)] + other
        to_far[r] = terms[r, 2].astype(jnp.bfloat16)
        send(four_down, to_far.at[r], from_far.at[r],
             rev_send.at[0, r], rev_recv.at[0, r], band, col - 2)
        left_sum[r] = own_left

    def return_near(r):
        @pl.when(both(two_down, two_up))
        def _():
            arrive(True, from_far.at[r], rev_send.at[0, r], rev_recv.at[0, r])
            terms[r, 1] = terms[r, 1] + from_far[r].astype(jnp.float32)

        to_near[r] = terms[r, 1].astype(jnp.bfloat16)
        send(two_down, to_near.at[r], from_near.at[r],
             rev_send.at[1, r], rev_recv.at[1, r], band, col - 2)

    def settle_left(r):
        arrive(True, from_partner.at[r], left_send.at[1, r], left_recv.at[1, r])
        total = left_sum[r] + from_partner[r].astype(jnp.float32)
        grad[0, r + 1, pl.ds(EDGE, columns)] = total.astype(jnp.bfloat16)

    def settle(r):
        @pl.when(two_up)
        def _():
            arrive(True, from_near.at[r], rev_send.at[1, r], rev_recv.at[1, r])
            terms[r, 0] = terms[r, 0] + from_near[r].astype(jnp.float32)

        grad[1, r + 1, pl.ds(EDGE, columns)] = terms[r, 0].astype(jnp.bfloat16)

    def grads_out(which):
        halo_out(
            lambda row, rows, first, count: grad.at[which, pl.ds(1 + row, rows), pl.ds(EDGE + first, count)],
            grad, 2 + which,
        )

    stages = ((pass_near, 0), (correlate, 1), (return_near, 3))
    for step in range(height + 3):
        for stage, lag in stages:
            if 0 <= step - lag < height:
                stage(step - lag)
        if step == height:
            for r in range(height):
                settle_left(r)
            grads_out(0)
    for r in range(height):
        settle(r)
    grads_out(1)
    halo_in(grad, 2)
    results[0] = convolve(grad, 0, True)
    out_left = pltpu.make_async_copy(results.at[0], gl_ref, local_sem.at[5])
    out_left.start()
    halo_in(grad, 3)
    results[1] = convolve(grad, 1, True)
    out_right = pltpu.make_async_copy(results.at[1], gr_ref, local_sem.at[6])
    out_right.start()
    for cond, describe in pending:
        guarded(cond, lambda: describe().wait_send())
    out_left.wait()
    out_right.wait()


def solution(mesh):
    bands, cols = mesh.shape["band"], mesh.shape["col"]

    def shards(left_image, right_image, weights, valid_mask, disparity):
        height, columns, channels = left_image.shape
        slots = DISP // columns // 2 + 1
        wide = columns + 2 * EDGE
        bf16 = jnp.bfloat16
        any_spec = pl.BlockSpec(memory_space=pl.ANY)
        dma = pltpu.SemaphoreType.DMA
        pad = pltpu.VMEM((2, height + 2, wide, channels), bf16)
        rows = pltpu.VMEM((height, columns, channels), bf16)
        both_rows = pltpu.VMEM((2, height, columns, channels), bf16)
        pixels = pltpu.VMEM((2, height, columns), jnp.int32)

        def body(*refs):
            kernel(bands, cols, *refs)

        grad_left, grad_right = pl.pallas_call(
            body,
            out_shape=(
                jax.ShapeDtypeStruct(left_image.shape, jnp.float32),
                jax.ShapeDtypeStruct(right_image.shape, jnp.float32),
            ),
            in_specs=[any_spec] * 5,
            out_specs=(any_spec, any_spec),
            scratch_shapes=[
                pad,
                pltpu.VMEM(weights.shape, bf16),
                pltpu.VMEM(weights.shape, bf16),
                pixels, pixels,
                pltpu.VMEM((height, slots, columns, channels), bf16),
                both_rows,
                pltpu.VMEM((height, columns, channels), jnp.float32),
                pad,
                pltpu.VMEM((height, slots, columns, channels), jnp.float32),
                pltpu.VMEM((2, height, columns, channels), jnp.float32),
                rows, rows, rows,
                rows, rows, rows,
                dma((7,)),
                dma((4, 8)), dma((4, 8)),
                dma((2, height)), dma((2, height)),
                dma((2, height)), dma((2, height)),
                dma((2, height)), dma((2, height)),
                dma((2,)), dma((2,)),
            ],
            compiler_params=pltpu.CompilerParams(
                collective_id=0, has_side_effects=True, vmem_limit_bytes=60 * 2**20
            ),
            cost_estimate=pl.CostEstimate(
                flops=5_000_000_000, bytes_accessed=4_000_000, transcendentals=400_000
            ),
        )(left_image, right_image, weights, valid_mask, disparity)
        return grad_left.astype(bf16), grad_right.astype(bf16)

    return jax.shard_map(
        shards,
        mesh=mesh,
        in_specs=(
            P("band", "col", None),
            P("band", "col", None),
            P(),
            P("band", "col"),
            P("band", "col"),
        ),
        out_specs=(P("band", "col", None), P("band", "col", None)),
        check_vma=False,
    )
```

```python
import jax
import jax.numpy as jnp
from jax import lax
from jax.experimental import pallas as pl
from jax.experimental.pallas import tpu as pltpu
from jax.sharding import PartitionSpec as P

DISP = 512
EDGE = 16
MESH = pl.DeviceIdType.MESH
SIDES = [(-1, 0), (1, 0), (0, -1), (0, 1), (-1, -1), (-1, 1), (1, -1), (1, 1)]
NT = (((1,), (1,)), ((), ()))
TN = (((0,), (0,)), ((), ()))


def guarded(cond, action):
    if cond is True:
        action()
    else:
        pl.when(cond)(action)


def both(first, second):
    if first is True:
        return second
    if second is True:
        return first
    return jnp.logical_and(first, second)


def kernel(
    bands, cols, left_ref, right_ref, kernel_ref, valid_ref, truth_ref, gl_ref, gr_ref,
    image, weights, flipped, truth, valid, seg, lfeat, left_sum, grad, terms, results,
    to_partner, to_far, to_near, from_partner, from_far, from_near,
    local_sem, halo_send, halo_recv, fwd_send, fwd_recv, rev_send, rev_recv,
    left_send, left_recv, side_send, side_recv,
):
    band = lax.axis_index("band")
    col = lax.axis_index("col")
    height, columns, channels = left_ref.shape
    slots = DISP // columns // 2 + 1
    wide = columns + 2 * EDGE
    factor = channels ** (-0.5)
    even = lax.rem(col, 2) == 0
    odd = jnp.logical_not(even)
    partner = jnp.where(even, col + 1, col - 1)
    images = (left_ref, right_ref)
    pending = []

    def inside(step_b, step_c):
        cond = True
        if step_b < 0:
            cond = both(cond, band + step_b >= 0)
        if step_b > 0:
            cond = both(cond, band + step_b < bands)
        if step_c < 0:
            cond = both(cond, col + step_c >= 0)
        if step_c > 0:
            cond = both(cond, col + step_c < cols)
        return cond

    def send(cond, src, dst, sem_out, sem_in, to_band, to_col):
        def describe():
            return pltpu.make_async_remote_copy(
                src_ref=src, dst_ref=dst, send_sem=sem_out, recv_sem=sem_in,
                device_id={"band": to_band, "col": to_col}, device_id_type=MESH,
            )

        guarded(cond, lambda: describe().start())
        pending.append((cond, describe))

    def arrive(cond, dst, sem_out, sem_in):
        def wait():
            pltpu.make_async_remote_copy(
                src_ref=dst, dst_ref=dst, send_sem=sem_out, recv_sem=sem_in,
                device_id={"band": band, "col": partner}, device_id_type=MESH,
            ).wait_recv()

        guarded(cond, wait)

    def send_span(step, size, edge):
        return (0, edge) if step < 0 else ((size - edge, edge) if step > 0 else (0, size))

    def land_span(step, size, edge):
        return (size + edge, edge) if step < 0 else ((0, edge) if step > 0 else (edge, size))

    def halo_out(source, pad, which, picked=SIDES):
        for side in picked:
            number = SIDES.index(side)
            row, rows = send_span(side[0], height, 1)
            first, count = send_span(side[1], columns, EDGE)
            to_row, _ = land_span(side[0], height, 1)
            to_first, _ = land_span(side[1], columns, EDGE)
            send(
                inside(*side),
                source(row, rows, first, count),
                pad.at[which % 2, pl.ds(to_row, rows), pl.ds(to_first, count)],
                halo_send.at[which, number], halo_recv.at[which, number],
                band + side[0], col + side[1],
            )

    def halo_in(pad, which):
        for number, side in enumerate(SIDES):
            to_row, rows = land_span(side[0], height, 1)
            to_first, count = land_span(side[1], columns, EDGE)
            arrive(
                inside(-side[0], -side[1]),
                pad.at[which % 2, pl.ds(to_row, rows), pl.ds(to_first, count)],
                halo_send.at[which, number], halo_recv.at[which, number],
            )

    def convolve(pad, which, backward):
        spans = ((0, EDGE + columns), (EDGE, columns), (EDGE, columns + EDGE))
        total = None
        for b in (1, 0, 2):
            side = 2 - b if backward else b
            first, count = spans[side]
            lines = jnp.concatenate(
                [
                    pad[which, pl.ds(2 - a if backward else a, height), pl.ds(first, count)]
                    .reshape(height * count, channels)
                    for a in range(3)
                ],
                1,
            )
            source = flipped if backward else weights
            blocks = jnp.concatenate(
                [source[pl.ds((3 * a + b) * channels, channels), :] for a in range(3)], 0
            )
            part = jnp.dot(lines, blocks, preferred_element_type=jnp.float32)
            if side != 1:
                part = pltpu.roll(part, (1 - side) % (height * count), 0)
            part = part.reshape(height, count, channels)
            part = part[:, EDGE:] if side == 0 else part[:, :columns]
            total = part if total is None else total + part
        return total

    core = (pl.ds(1, height), pl.ds(EDGE, columns))
    locals_in = [
        pltpu.make_async_copy(right_ref, image.at[(1,) + core], local_sem.at[0]),
        pltpu.make_async_copy(left_ref, image.at[(0,) + core], local_sem.at[1]),
        pltpu.make_async_copy(kernel_ref, weights, local_sem.at[2]),
        pltpu.make_async_copy(truth_ref, truth.at[0], local_sem.at[3]),
        pltpu.make_async_copy(valid_ref, valid.at[0], local_sem.at[4]),
    ]
    for copy in locals_in:
        copy.start()

    for pad in (image, grad):
        for which in range(2):
            for row in (0, height + 1):
                pad[which, row] = jnp.zeros((wide, channels), jnp.bfloat16)
            for first in (0, EDGE + columns):
                pad[which, 1 : height + 1, first : first + EDGE] = jnp.zeros(
                    (height, EDGE, channels), jnp.bfloat16
                )
    for k in range(1, slots):
        @pl.when(col < 2 * k)
        def _(k=k):
            seg[:, k] = jnp.zeros((height, columns, channels), jnp.bfloat16)

    barrier = pltpu.get_barrier_semaphore()
    met = jnp.int32(0)
    for side in SIDES + [(0, -2), (0, 2)]:
        cond = inside(*side)

        def greet(side=side):
            pl.semaphore_signal(
                barrier, inc=1,
                device_id={"band": band + side[0], "col": col + side[1]}, device_id_type=MESH,
            )

        guarded(cond, greet)
        met = met + cond.astype(jnp.int32)
    pl.semaphore_wait(barrier, met)

    for which in (1, 0):
        halo_out(
            lambda row, rows, first, count: images[which].at[pl.ds(row, rows), pl.ds(first, count)],
            image, which,
        )
    send(True, truth_ref, truth.at[1], side_send.at[0], side_recv.at[0], band, partner)
    send(True, valid_ref, valid.at[1], side_send.at[1], side_recv.at[1], band, partner)
    locals_in[0].wait()
    locals_in[2].wait()
    for position in range(9):
        place = pl.ds(position * channels, channels)
        flipped[place, :] = weights[place, :].T
    halo_in(image, 1)
    seg[:, 0] = convolve(image, 1, False).astype(jnp.bfloat16)

    two_down, four_down = col >= 2, col >= 4
    two_up = col + 2 < cols

    def own_up(r):
        send(two_up, seg.at[r, 0], seg.at[r, 1], fwd_send.at[0, r], fwd_recv.at[0, r], band, col + 2)

    own_up(0)
    own_up(1)
    locals_in[1].wait()
    halo_in(image, 0)
    lfeat[0] = convolve(image, 0, False).astype(jnp.bfloat16)
    for r in range(height):
        send(True, lfeat.at[0, r], lfeat.at[1, r], left_send.at[0, r], left_recv.at[0, r], band, partner)
    for copy in locals_in[3:]:
        copy.wait()
    arrive(True, truth.at[1], side_send.at[0], side_recv.at[0])
    arrive(True, valid.at[1], side_send.at[1], side_recv.at[1])

    odd_slot = odd.astype(jnp.int32)

    def pass_near(r):
        arrive(two_down, seg.at[r, 1], fwd_send.at[0, r], fwd_recv.at[0, r])
        send(both(two_down, two_up), seg.at[r, 1], seg.at[r, 2],
             fwd_send.at[1, r], fwd_recv.at[1, r], band, col + 2)
        if r + 2 < height:
            own_up(r + 2)

    def slopes(r, who, block, first, count):
        shape = (count, columns, columns)
        offset = (
            (2 * lax.broadcasted_iota(jnp.int32, shape, 0) + first) * columns
            + lax.broadcasted_iota(jnp.int32, shape, 2)
            - lax.broadcasted_iota(jnp.int32, shape, 1)
        )
        left = lfeat[who, r]
        scores = lax.dot_general(block, left, NT, preferred_element_type=jnp.float32) * factor
        scores = scores.reshape(shape)
        distance = (offset - truth[who, r : r + 1, :].reshape(1, 1, columns)).astype(jnp.float32)
        target = jnp.exp(distance * distance * (-1.0 / 8.0))
        scale = valid[who, r : r + 1, :].astype(jnp.float32).reshape(1, 1, columns)
        slope = scale * (scores - target) * (channels / DISP)
        slope = jnp.where(jnp.logical_and(offset >= 0, offset < DISP), slope, 0.0)
        slope = slope.astype(jnp.bfloat16).reshape(count * columns, columns)
        term = jnp.dot(slope, left, preferred_element_type=jnp.float32) * factor
        dleft = lax.dot_general(slope, block, TN, preferred_element_type=jnp.float32) * factor
        return term.reshape(count, columns, channels), dleft

    def correlate(r):
        arrive(four_down, seg.at[r, 2], fwd_send.at[1, r], fwd_recv.at[1, r])
        arrive(True, lfeat.at[1, r], left_send.at[0, r], left_recv.at[0, r])
        block = seg[r, pl.ds(odd_slot, slots - 1)].reshape((slots - 1) * columns, channels)
        other, other_left = slopes(r, 1, block, 1, slots - 1)
        to_partner[r] = other_left.astype(jnp.bfloat16)
        send(True, to_partner.at[r], from_partner.at[r],
             left_send.at[1, r], left_recv.at[1, r], band, partner)
        own, own_left = slopes(r, 0, seg[r].reshape(slots * columns, channels), 0, slots)
        terms[r] = own
        terms[r, pl.ds(odd_slot, slots - 1)] = terms[r, pl.ds(odd_slot, slots - 1)] + other
        to_far[r] = terms[r, 2].astype(jnp.bfloat16)
        send(four_down, to_far.at[r], from_far.at[r],
             rev_send.at[0, r], rev_recv.at[0, r], band, col - 2)
        left_sum[r] = own_left

    def return_near(r):
        @pl.when(both(two_down, two_up))
        def _():
            arrive(True, from_far.at[r], rev_send.at[0, r], rev_recv.at[0, r])
            terms[r, 1] = terms[r, 1] + from_far[r].astype(jnp.float32)

        to_near[r] = terms[r, 1].astype(jnp.bfloat16)
        send(two_down, to_near.at[r], from_near.at[r],
             rev_send.at[1, r], rev_recv.at[1, r], band, col - 2)

    def settle_left(r):
        arrive(True, from_partner.at[r], left_send.at[1, r], left_recv.at[1, r])
        total = left_sum[r] + from_partner[r].astype(jnp.float32)
        grad[0, r + 1, pl.ds(EDGE, columns)] = total.astype(jnp.bfloat16)

    def settle(r):
        @pl.when(two_up)
        def _():
            arrive(True, from_near.at[r], rev_send.at[1, r], rev_recv.at[1, r])
            terms[r, 0] = terms[r, 0] + from_near[r].astype(jnp.float32)

        grad[1, r + 1, pl.ds(EDGE, columns)] = terms[r, 0].astype(jnp.bfloat16)

    def grads_out(which):
        halo_out(
            lambda row, rows, first, count: grad.at[which, pl.ds(1 + row, rows), pl.ds(EDGE + first, count)],
            grad, 2 + which,
        )

    stages = ((pass_near, 0), (correlate, 1), (return_near, 3))
    for step in range(height + 3):
        for stage, lag in stages:
            if 0 <= step - lag < height:
                stage(step - lag)
        if step == height:
            for r in range(height):
                settle_left(r)
            grads_out(0)
    for r in range(height):
        settle(r)
    grads_out(1)
    halo_in(grad, 2)
    results[0] = convolve(grad, 0, True).astype(jnp.bfloat16)
    out_left = pltpu.make_async_copy(results.at[0], gl_ref, local_sem.at[5])
    out_left.start()
    halo_in(grad, 3)
    results[1] = convolve(grad, 1, True).astype(jnp.bfloat16)
    out_right = pltpu.make_async_copy(results.at[1], gr_ref, local_sem.at[6])
    out_right.start()
    for cond, describe in pending:
        guarded(cond, lambda: describe().wait_send())
    out_left.wait()
    out_right.wait()


def hand_out(left_ref, right_ref, gl_ref, gr_ref, sems):
    height = left_ref.shape[0]
    copies = [
        pltpu.make_async_copy(source.at[r], target.at[r], sems.at[which, r])
        for r in range(height)
        for which, (source, target) in enumerate(((left_ref, gl_ref), (right_ref, gr_ref)))
    ]
    for copy in copies:
        copy.start()
    for copy in copies:
        copy.wait()


def solution(mesh):
    bands, cols = mesh.shape["band"], mesh.shape["col"]

    def shards(left_image, right_image, weights, valid_mask, disparity):
        height, columns, channels = left_image.shape
        slots = DISP // columns // 2 + 1
        wide = columns + 2 * EDGE
        bf16 = jnp.bfloat16
        any_spec = pl.BlockSpec(memory_space=pl.ANY)
        dma = pltpu.SemaphoreType.DMA
        pad = pltpu.VMEM((2, height + 2, wide, channels), bf16)
        rows = pltpu.VMEM((height, columns, channels), bf16)
        both_rows = pltpu.VMEM((2, height, columns, channels), bf16)
        pixels = pltpu.VMEM((2, height, columns), jnp.int32)

        def body(*refs):
            kernel(bands, cols, *refs)

        grad_left, grad_right = pl.pallas_call(
            body,
            out_shape=(
                jax.ShapeDtypeStruct(left_image.shape, bf16),
                jax.ShapeDtypeStruct(right_image.shape, bf16),
            ),
            in_specs=[any_spec] * 5,
            out_specs=(any_spec, any_spec),
            scratch_shapes=[
                pad,
                pltpu.VMEM(weights.shape, bf16),
                pltpu.VMEM(weights.shape, bf16),
                pixels, pixels,
                pltpu.VMEM((height, slots, columns, channels), bf16),
                both_rows,
                pltpu.VMEM((height, columns, channels), jnp.float32),
                pad,
                pltpu.VMEM((height, slots, columns, channels), jnp.float32),
                both_rows,
                rows, rows, rows,
                rows, rows, rows,
                dma((7,)),
                dma((4, 8)), dma((4, 8)),
                dma((2, height)), dma((2, height)),
                dma((2, height)), dma((2, height)),
                dma((2, height)), dma((2, height)),
                dma((2,)), dma((2,)),
            ],
            compiler_params=pltpu.CompilerParams(
                collective_id=0, has_side_effects=True, vmem_limit_bytes=60 * 2**20
            ),
            cost_estimate=pl.CostEstimate(
                flops=5_000_000_000, bytes_accessed=4_000_000, transcendentals=400_000
            ),
        )(left_image, right_image, weights, valid_mask, disparity)
        return pl.pallas_call(
            hand_out,
            out_shape=(
                jax.ShapeDtypeStruct(left_image.shape, bf16),
                jax.ShapeDtypeStruct(right_image.shape, bf16),
            ),
            in_specs=[any_spec, any_spec],
            out_specs=(any_spec, any_spec),
            scratch_shapes=[dma((2, height))],
            compiler_params=pltpu.CompilerParams(vmem_limit_bytes=60 * 2**20),
        )(grad_left, grad_right)

    return jax.shard_map(
        shards,
        mesh=mesh,
        in_specs=(
            P("band", "col", None),
            P("band", "col", None),
            P(),
            P("band", "col"),
            P("band", "col"),
        ),
        out_specs=(P("band", "col", None), P("band", "col", None)),
        check_vma=False,
    )
```

```python
import jax
import jax.numpy as jnp
from jax import lax
from jax.experimental import pallas as pl
from jax.experimental.pallas import tpu as pltpu
from jax.sharding import PartitionSpec as P

DISP = 512
EDGE = 16
MESH = pl.DeviceIdType.MESH
SIDES = [(-1, 0), (1, 0), (0, -1), (0, 1), (-1, -1), (-1, 1), (1, -1), (1, 1)]
NT = (((1,), (1,)), ((), ()))
TN = (((0,), (0,)), ((), ()))


def guarded(cond, action):
    if cond is True:
        action()
    else:
        pl.when(cond)(action)


def both(first, second):
    if first is True:
        return second
    if second is True:
        return first
    return jnp.logical_and(first, second)


def kernel(
    bands, cols, left_ref, right_ref, kernel_ref, valid_ref, truth_ref, gl_ref, gr_ref,
    image, weights, flipped, truth, valid, seg, lfeat, left_sum, grad, terms, results,
    to_partner, to_far, to_near, from_partner, from_far, from_near,
    local_sem, halo_send, halo_recv, fwd_send, fwd_recv, rev_send, rev_recv,
    left_send, left_recv, side_send, side_recv,
):
    band = lax.axis_index("band")
    col = lax.axis_index("col")
    height, columns, channels = left_ref.shape
    slots = DISP // columns // 2 + 1
    wide = columns + 2 * EDGE
    factor = channels ** (-0.5)
    even = lax.rem(col, 2) == 0
    odd = jnp.logical_not(even)
    partner = jnp.where(even, col + 1, col - 1)
    pending = []

    def inside(step_b, step_c):
        cond = True
        if step_b < 0:
            cond = both(cond, band + step_b >= 0)
        if step_b > 0:
            cond = both(cond, band + step_b < bands)
        if step_c < 0:
            cond = both(cond, col + step_c >= 0)
        if step_c > 0:
            cond = both(cond, col + step_c < cols)
        return cond

    def send(cond, src, dst, sem_out, sem_in, to_band, to_col):
        def describe():
            return pltpu.make_async_remote_copy(
                src_ref=src, dst_ref=dst, send_sem=sem_out, recv_sem=sem_in,
                device_id={"band": to_band, "col": to_col}, device_id_type=MESH,
            )

        guarded(cond, lambda: describe().start())
        pending.append((cond, describe))

    def arrive(cond, dst, sem_out, sem_in):
        def wait():
            pltpu.make_async_remote_copy(
                src_ref=dst, dst_ref=dst, send_sem=sem_out, recv_sem=sem_in,
                device_id={"band": band, "col": partner}, device_id_type=MESH,
            ).wait_recv()

        guarded(cond, wait)

    def send_span(step, size, edge):
        return (0, edge) if step < 0 else ((size - edge, edge) if step > 0 else (0, size))

    def land_span(step, size, edge):
        return (size + edge, edge) if step < 0 else ((0, edge) if step > 0 else (edge, size))

    def halo_out(source, pad, which, picked=SIDES):
        for side in picked:
            number = SIDES.index(side)
            row, rows = send_span(side[0], height, 1)
            first, count = send_span(side[1], columns, EDGE)
            to_row, _ = land_span(side[0], height, 1)
            to_first, _ = land_span(side[1], columns, EDGE)
            send(
                inside(*side),
                source(row, rows, first, count),
                pad.at[which % 2, pl.ds(to_row, rows), pl.ds(to_first, count)],
                halo_send.at[which, number], halo_recv.at[which, number],
                band + side[0], col + side[1],
            )

    def halo_in(pad, which):
        for number, side in enumerate(SIDES):
            to_row, rows = land_span(side[0], height, 1)
            to_first, count = land_span(side[1], columns, EDGE)
            arrive(
                inside(-side[0], -side[1]),
                pad.at[which % 2, pl.ds(to_row, rows), pl.ds(to_first, count)],
                halo_send.at[which, number], halo_recv.at[which, number],
            )

    def convolve(pad, which, backward):
        spans = ((0, EDGE + columns), (EDGE, columns), (EDGE, columns + EDGE))
        total = None
        for b in (1, 0, 2):
            side = 2 - b if backward else b
            first, count = spans[side]
            lines = jnp.concatenate(
                [
                    pad[which, pl.ds(2 - a if backward else a, height), pl.ds(first, count)]
                    .reshape(height * count, channels)
                    for a in range(3)
                ],
                1,
            )
            source = flipped if backward else weights
            blocks = jnp.concatenate(
                [source[pl.ds((3 * a + b) * channels, channels), :] for a in range(3)], 0
            )
            part = jnp.dot(lines, blocks, preferred_element_type=jnp.float32)
            if side != 1:
                part = pltpu.roll(part, (1 - side) % (height * count), 0)
            part = part.reshape(height, count, channels)
            part = part[:, EDGE:] if side == 0 else part[:, :columns]
            total = part if total is None else total + part
        return total

    core = (pl.ds(1, height), pl.ds(EDGE, columns))
    locals_in = [
        pltpu.make_async_copy(right_ref, image.at[(1,) + core], local_sem.at[0]),
        pltpu.make_async_copy(left_ref, image.at[(0,) + core], local_sem.at[1]),
        pltpu.make_async_copy(kernel_ref, weights, local_sem.at[2]),
        pltpu.make_async_copy(truth_ref, truth.at[0], local_sem.at[3]),
        pltpu.make_async_copy(valid_ref, valid.at[0], local_sem.at[4]),
    ]
    for copy in locals_in:
        copy.start()

    for pad in (image, grad):
        for which in range(2):
            for row in (0, height + 1):
                pad[which, row] = jnp.zeros((wide, channels), jnp.bfloat16)
            for first in (0, EDGE + columns):
                pad[which, 1 : height + 1, first : first + EDGE] = jnp.zeros(
                    (height, EDGE, channels), jnp.bfloat16
                )
    for k in range(1, slots):
        @pl.when(col < 2 * k)
        def _(k=k):
            seg[:, k] = jnp.zeros((height, columns, channels), jnp.bfloat16)

    barrier = pltpu.get_barrier_semaphore()
    met = jnp.int32(0)
    for side in SIDES + [(0, -2), (0, 2)]:
        cond = inside(*side)

        def greet(side=side):
            pl.semaphore_signal(
                barrier, inc=1,
                device_id={"band": band + side[0], "col": col + side[1]}, device_id_type=MESH,
            )

        guarded(cond, greet)
        met = met + cond.astype(jnp.int32)
    pl.semaphore_wait(barrier, met)

    def images_out(which):
        halo_out(
            lambda row, rows, first, count: image.at[which, pl.ds(1 + row, rows), pl.ds(EDGE + first, count)],
            image, which,
        )

    for which in (1, 0):
        locals_in[1 - which].wait()
        images_out(which)
    for copy in locals_in[2:]:
        copy.wait()
    send(True, truth.at[0], truth.at[1], side_send.at[0], side_recv.at[0], band, partner)
    send(True, valid.at[0], valid.at[1], side_send.at[1], side_recv.at[1], band, partner)
    for position in range(9):
        place = pl.ds(position * channels, channels)
        flipped[place, :] = weights[place, :].T
    halo_in(image, 1)
    seg[:, 0] = convolve(image, 1, False).astype(jnp.bfloat16)

    two_down, four_down = col >= 2, col >= 4
    two_up = col + 2 < cols

    def own_up(r):
        send(two_up, seg.at[r, 0], seg.at[r, 1], fwd_send.at[0, r], fwd_recv.at[0, r], band, col + 2)

    own_up(0)
    own_up(1)
    halo_in(image, 0)
    lfeat[0] = convolve(image, 0, False).astype(jnp.bfloat16)
    for r in range(height):
        send(True, lfeat.at[0, r], lfeat.at[1, r], left_send.at[0, r], left_recv.at[0, r], band, partner)
    arrive(True, truth.at[1], side_send.at[0], side_recv.at[0])
    arrive(True, valid.at[1], side_send.at[1], side_recv.at[1])

    odd_slot = odd.astype(jnp.int32)

    def pass_near(r):
        arrive(two_down, seg.at[r, 1], fwd_send.at[0, r], fwd_recv.at[0, r])
        send(both(two_down, two_up), seg.at[r, 1], seg.at[r, 2],
             fwd_send.at[1, r], fwd_recv.at[1, r], band, col + 2)
        if r + 2 < height:
            own_up(r + 2)

    def slopes(r, who, block, first, count):
        shape = (count, columns, columns)
        offset = (
            (2 * lax.broadcasted_iota(jnp.int32, shape, 0) + first) * columns
            + lax.broadcasted_iota(jnp.int32, shape, 2)
            - lax.broadcasted_iota(jnp.int32, shape, 1)
        )
        left = lfeat[who, r]
        scores = lax.dot_general(block, left, NT, preferred_element_type=jnp.float32) * factor
        scores = scores.reshape(shape)
        distance = (offset - truth[who, r : r + 1, :].reshape(1, 1, columns)).astype(jnp.float32)
        target = jnp.exp(distance * distance * (-1.0 / 8.0))
        scale = valid[who, r : r + 1, :].astype(jnp.float32).reshape(1, 1, columns)
        slope = scale * (scores - target) * (channels / DISP)
        slope = jnp.where(jnp.logical_and(offset >= 0, offset < DISP), slope, 0.0)
        slope = slope.astype(jnp.bfloat16).reshape(count * columns, columns)
        term = jnp.dot(slope, left, preferred_element_type=jnp.float32) * factor
        dleft = lax.dot_general(slope, block, TN, preferred_element_type=jnp.float32) * factor
        return term.reshape(count, columns, channels), dleft

    def correlate(r):
        arrive(four_down, seg.at[r, 2], fwd_send.at[1, r], fwd_recv.at[1, r])
        arrive(True, lfeat.at[1, r], left_send.at[0, r], left_recv.at[0, r])
        block = seg[r, pl.ds(odd_slot, slots - 1)].reshape((slots - 1) * columns, channels)
        other, other_left = slopes(r, 1, block, 1, slots - 1)
        to_partner[r] = other_left.astype(jnp.bfloat16)
        send(True, to_partner.at[r], from_partner.at[r],
             left_send.at[1, r], left_recv.at[1, r], band, partner)
        own, own_left = slopes(r, 0, seg[r].reshape(slots * columns, channels), 0, slots)
        terms[r] = own
        terms[r, pl.ds(odd_slot, slots - 1)] = terms[r, pl.ds(odd_slot, slots - 1)] + other
        to_far[r] = terms[r, 2].astype(jnp.bfloat16)
        send(four_down, to_far.at[r], from_far.at[r],
             rev_send.at[0, r], rev_recv.at[0, r], band, col - 2)
        left_sum[r] = own_left

    def return_near(r):
        @pl.when(both(two_down, two_up))
        def _():
            arrive(True, from_far.at[r], rev_send.at[0, r], rev_recv.at[0, r])
            terms[r, 1] = terms[r, 1] + from_far[r].astype(jnp.float32)

        to_near[r] = terms[r, 1].astype(jnp.bfloat16)
        send(two_down, to_near.at[r], from_near.at[r],
             rev_send.at[1, r], rev_recv.at[1, r], band, col - 2)

    def settle_left(r):
        arrive(True, from_partner.at[r], left_send.at[1, r], left_recv.at[1, r])
        total = left_sum[r] + from_partner[r].astype(jnp.float32)
        grad[0, r + 1, pl.ds(EDGE, columns)] = total.astype(jnp.bfloat16)

    def settle(r):
        @pl.when(two_up)
        def _():
            arrive(True, from_near.at[r], rev_send.at[1, r], rev_recv.at[1, r])
            terms[r, 0] = terms[r, 0] + from_near[r].astype(jnp.float32)

        grad[1, r + 1, pl.ds(EDGE, columns)] = terms[r, 0].astype(jnp.bfloat16)

    def grads_out(which):
        halo_out(
            lambda row, rows, first, count: grad.at[which, pl.ds(1 + row, rows), pl.ds(EDGE + first, count)],
            grad, 2 + which,
        )

    stages = ((pass_near, 0), (correlate, 1), (return_near, 3))
    for step in range(height + 3):
        for stage, lag in stages:
            if 0 <= step - lag < height:
                stage(step - lag)
        if step == height:
            for r in range(height):
                settle_left(r)
            grads_out(0)
    for r in range(height):
        settle(r)
    grads_out(1)
    halo_in(grad, 2)
    results[0] = convolve(grad, 0, True).astype(jnp.bfloat16)
    out_left = pltpu.make_async_copy(results.at[0], gl_ref, local_sem.at[5])
    out_left.start()
    halo_in(grad, 3)
    results[1] = convolve(grad, 1, True).astype(jnp.bfloat16)
    out_right = pltpu.make_async_copy(results.at[1], gr_ref, local_sem.at[6])
    out_right.start()
    for cond, describe in pending:
        guarded(cond, lambda: describe().wait_send())
    out_left.wait()
    out_right.wait()


def hand_out(left_ref, right_ref, gl_ref, gr_ref):
    gl_ref[...] = left_ref[...]
    gr_ref[...] = right_ref[...]


def solution(mesh):
    bands, cols = mesh.shape["band"], mesh.shape["col"]

    def shards(left_image, right_image, weights, valid_mask, disparity):
        height, columns, channels = left_image.shape
        slots = DISP // columns // 2 + 1
        wide = columns + 2 * EDGE
        bf16 = jnp.bfloat16
        vmem_spec = pl.BlockSpec(memory_space=pltpu.VMEM)
        any_spec = pl.BlockSpec(memory_space=pl.ANY)
        dma = pltpu.SemaphoreType.DMA
        pad = pltpu.VMEM((2, height + 2, wide, channels), bf16)
        rows = pltpu.VMEM((height, columns, channels), bf16)
        both_rows = pltpu.VMEM((2, height, columns, channels), bf16)
        pixels = pltpu.VMEM((2, height, columns), jnp.int32)

        def body(*refs):
            kernel(bands, cols, *refs)

        grad_left, grad_right = pl.pallas_call(
            body,
            out_shape=(
                jax.ShapeDtypeStruct(left_image.shape, bf16),
                jax.ShapeDtypeStruct(right_image.shape, bf16),
            ),
            in_specs=[any_spec] * 5,
            out_specs=(any_spec, any_spec),
            scratch_shapes=[
                pad,
                pltpu.VMEM(weights.shape, bf16),
                pltpu.VMEM(weights.shape, bf16),
                pixels, pixels,
                pltpu.VMEM((height, slots, columns, channels), bf16),
                both_rows,
                pltpu.VMEM((height, columns, channels), jnp.float32),
                pad,
                pltpu.VMEM((height, slots, columns, channels), jnp.float32),
                both_rows,
                rows, rows, rows,
                rows, rows, rows,
                dma((7,)),
                dma((4, 8)), dma((4, 8)),
                dma((2, height)), dma((2, height)),
                dma((2, height)), dma((2, height)),
                dma((2, height)), dma((2, height)),
                dma((2,)), dma((2,)),
            ],
            compiler_params=pltpu.CompilerParams(
                collective_id=0, has_side_effects=True, vmem_limit_bytes=60 * 2**20
            ),
            cost_estimate=pl.CostEstimate(
                flops=5_000_000_000, bytes_accessed=4_000_000, transcendentals=400_000
            ),
        )(left_image, right_image, weights, valid_mask, disparity)
        return pl.pallas_call(
            hand_out,
            out_shape=(
                jax.ShapeDtypeStruct(left_image.shape, bf16),
                jax.ShapeDtypeStruct(right_image.shape, bf16),
            ),
            in_specs=[vmem_spec, vmem_spec],
            out_specs=(vmem_spec, vmem_spec),
            compiler_params=pltpu.CompilerParams(vmem_limit_bytes=60 * 2**20),
        )(grad_left, grad_right)

    return jax.shard_map(
        shards,
        mesh=mesh,
        in_specs=(
            P("band", "col", None),
            P("band", "col", None),
            P(),
            P("band", "col"),
            P("band", "col"),
        ),
        out_specs=(P("band", "col", None), P("band", "col", None)),
        check_vma=False,
    )
```

```python
import jax
import jax.numpy as jnp
from jax import lax
from jax.experimental import pallas as pl
from jax.experimental.pallas import tpu as pltpu
from jax.sharding import PartitionSpec as P

DISP = 512
EDGE = 16
MESH = pl.DeviceIdType.MESH
SIDES = [(-1, 0), (1, 0), (0, -1), (0, 1), (-1, -1), (-1, 1), (1, -1), (1, 1)]
NT = (((1,), (1,)), ((), ()))
TN = (((0,), (0,)), ((), ()))


def guarded(cond, action):
    if cond is True:
        action()
    else:
        pl.when(cond)(action)


def both(first, second):
    if first is True:
        return second
    if second is True:
        return first
    return jnp.logical_and(first, second)


def kernel(
    bands, cols, left_ref, right_ref, kernel_ref, valid_ref, truth_ref, gl_ref, gr_ref,
    image, weights, flipped, truth, valid, seg, lfeat, left_sum, grad, terms, results,
    to_partner, to_far, to_near, from_partner, from_far, from_near,
    local_sem, halo_send, halo_recv, fwd_send, fwd_recv, rev_send, rev_recv,
    left_send, left_recv, side_send, side_recv,
):
    band = lax.axis_index("band")
    col = lax.axis_index("col")
    height, columns, channels = left_ref.shape
    slots = DISP // columns // 2 + 1
    wide = columns + 2 * EDGE
    factor = channels ** (-0.5)
    even = lax.rem(col, 2) == 0
    odd = jnp.logical_not(even)
    partner = jnp.where(even, col + 1, col - 1)
    pending = []

    def inside(step_b, step_c):
        cond = True
        if step_b < 0:
            cond = both(cond, band + step_b >= 0)
        if step_b > 0:
            cond = both(cond, band + step_b < bands)
        if step_c < 0:
            cond = both(cond, col + step_c >= 0)
        if step_c > 0:
            cond = both(cond, col + step_c < cols)
        return cond

    def send(cond, src, dst, sem_out, sem_in, to_band, to_col):
        def describe():
            return pltpu.make_async_remote_copy(
                src_ref=src, dst_ref=dst, send_sem=sem_out, recv_sem=sem_in,
                device_id={"band": to_band, "col": to_col}, device_id_type=MESH,
            )

        guarded(cond, lambda: describe().start())
        pending.append((cond, describe))

    def arrive(cond, dst, sem_out, sem_in):
        def wait():
            pltpu.make_async_remote_copy(
                src_ref=dst, dst_ref=dst, send_sem=sem_out, recv_sem=sem_in,
                device_id={"band": band, "col": partner}, device_id_type=MESH,
            ).wait_recv()

        guarded(cond, wait)

    def send_span(step, size, edge):
        return (0, edge) if step < 0 else ((size - edge, edge) if step > 0 else (0, size))

    def land_span(step, size, edge):
        return (size + edge, edge) if step < 0 else ((0, edge) if step > 0 else (edge, size))

    def halo_out(source, pad, which, picked=SIDES):
        for side in picked:
            number = SIDES.index(side)
            row, rows = send_span(side[0], height, 1)
            first, count = send_span(side[1], columns, EDGE)
            to_row, _ = land_span(side[0], height, 1)
            to_first, _ = land_span(side[1], columns, EDGE)
            send(
                inside(*side),
                source(row, rows, first, count),
                pad.at[which % 2, pl.ds(to_row, rows), pl.ds(to_first, count)],
                halo_send.at[which, number], halo_recv.at[which, number],
                band + side[0], col + side[1],
            )

    def halo_in(pad, which):
        for number, side in enumerate(SIDES):
            to_row, rows = land_span(side[0], height, 1)
            to_first, count = land_span(side[1], columns, EDGE)
            arrive(
                inside(-side[0], -side[1]),
                pad.at[which % 2, pl.ds(to_row, rows), pl.ds(to_first, count)],
                halo_send.at[which, number], halo_recv.at[which, number],
            )

    def convolve(pad, which, backward):
        spans = ((0, EDGE + columns), (EDGE, columns), (EDGE, columns + EDGE))
        total = None
        for b in (1, 0, 2):
            side = 2 - b if backward else b
            first, count = spans[side]
            lines = jnp.concatenate(
                [
                    pad[which, pl.ds(2 - a if backward else a, height), pl.ds(first, count)]
                    .reshape(height * count, channels)
                    for a in range(3)
                ],
                1,
            )
            source = flipped if backward else weights
            blocks = jnp.concatenate(
                [source[pl.ds((3 * a + b) * channels, channels), :] for a in range(3)], 0
            )
            part = jnp.dot(lines, blocks, preferred_element_type=jnp.float32)
            if side != 1:
                part = pltpu.roll(part, (1 - side) % (height * count), 0)
            part = part.reshape(height, count, channels)
            part = part[:, EDGE:] if side == 0 else part[:, :columns]
            total = part if total is None else total + part
        return total

    core = (pl.ds(1, height), pl.ds(EDGE, columns))
    locals_in = [
        pltpu.make_async_copy(right_ref, image.at[(1,) + core], local_sem.at[0]),
        pltpu.make_async_copy(left_ref, image.at[(0,) + core], local_sem.at[1]),
        pltpu.make_async_copy(kernel_ref, weights, local_sem.at[2]),
        pltpu.make_async_copy(truth_ref, truth.at[0], local_sem.at[3]),
        pltpu.make_async_copy(valid_ref, valid.at[0], local_sem.at[4]),
    ]
    for copy in locals_in:
        copy.start()

    for pad in (image, grad):
        for which in range(2):
            for row in (0, height + 1):
                pad[which, row] = jnp.zeros((wide, channels), jnp.bfloat16)
            for first in (0, EDGE + columns):
                pad[which, 1 : height + 1, first : first + EDGE] = jnp.zeros(
                    (height, EDGE, channels), jnp.bfloat16
                )
    for k in range(1, slots):
        @pl.when(col < 2 * k)
        def _(k=k):
            seg[:, k] = jnp.zeros((height, columns, channels), jnp.bfloat16)

    barrier = pltpu.get_barrier_semaphore()
    met = jnp.int32(0)
    for side in SIDES + [(0, -2), (0, 2)]:
        cond = inside(*side)

        def greet(side=side):
            pl.semaphore_signal(
                barrier, inc=1,
                device_id={"band": band + side[0], "col": col + side[1]}, device_id_type=MESH,
            )

        guarded(cond, greet)
        met = met + cond.astype(jnp.int32)
    pl.semaphore_wait(barrier, met)

    def images_out(which):
        halo_out(
            lambda row, rows, first, count: image.at[which, pl.ds(1 + row, rows), pl.ds(EDGE + first, count)],
            image, which,
        )

    for which in (1, 0):
        locals_in[1 - which].wait()
        images_out(which)
    for copy in locals_in[2:]:
        copy.wait()
    send(True, truth.at[0], truth.at[1], side_send.at[0], side_recv.at[0], band, partner)
    send(True, valid.at[0], valid.at[1], side_send.at[1], side_recv.at[1], band, partner)
    halo_in(image, 1)
    seg[:, 0] = convolve(image, 1, False).astype(jnp.bfloat16)

    two_down, four_down = col >= 2, col >= 4
    two_up = col + 2 < cols

    def own_up(r):
        send(two_up, seg.at[r, 0], seg.at[r, 1], fwd_send.at[0, r], fwd_recv.at[0, r], band, col + 2)

    own_up(0)
    own_up(1)
    halo_in(image, 0)
    lfeat[0] = convolve(image, 0, False).astype(jnp.bfloat16)
    for r in range(height):
        send(True, lfeat.at[0, r], lfeat.at[1, r], left_send.at[0, r], left_recv.at[0, r], band, partner)
    for position in range(9):
        place = pl.ds(position * channels, channels)
        flipped[place, :] = weights[place, :].T
    arrive(True, truth.at[1], side_send.at[0], side_recv.at[0])
    arrive(True, valid.at[1], side_send.at[1], side_recv.at[1])

    odd_slot = odd.astype(jnp.int32)

    def pass_near(r):
        arrive(two_down, seg.at[r, 1], fwd_send.at[0, r], fwd_recv.at[0, r])
        send(both(two_down, two_up), seg.at[r, 1], seg.at[r, 2],
             fwd_send.at[1, r], fwd_recv.at[1, r], band, col + 2)
        if r + 2 < height:
            own_up(r + 2)

    def slopes(r, who, block, first, count):
        shape = (count, columns, columns)
        offset = (
            (2 * lax.broadcasted_iota(jnp.int32, shape, 0) + first) * columns
            + lax.broadcasted_iota(jnp.int32, shape, 2)
            - lax.broadcasted_iota(jnp.int32, shape, 1)
        )
        left = lfeat[who, r]
        scores = lax.dot_general(block, left, NT, preferred_element_type=jnp.float32) * factor
        scores = scores.reshape(shape)
        distance = (offset - truth[who, r : r + 1, :].reshape(1, 1, columns)).astype(jnp.float32)
        target = jnp.exp(distance * distance * (-1.0 / 8.0))
        scale = valid[who, r : r + 1, :].astype(jnp.float32).reshape(1, 1, columns)
        slope = scale * (scores - target) * (channels / DISP)
        slope = jnp.where(jnp.logical_and(offset >= 0, offset < DISP), slope, 0.0)
        slope = slope.astype(jnp.bfloat16).reshape(count * columns, columns)
        term = jnp.dot(slope, left, preferred_element_type=jnp.float32) * factor
        return term.reshape(count, columns, channels), slope

    def pull(slope, block):
        return lax.dot_general(slope, block, TN, preferred_element_type=jnp.float32) * factor

    def correlate(r):
        arrive(four_down, seg.at[r, 2], fwd_send.at[1, r], fwd_recv.at[1, r])
        arrive(True, lfeat.at[1, r], left_send.at[0, r], left_recv.at[0, r])
        block = seg[r, pl.ds(odd_slot, slots - 1)].reshape((slots - 1) * columns, channels)
        other, other_slope = slopes(r, 1, block, 1, slots - 1)
        whole = seg[r].reshape(slots * columns, channels)
        own, own_slope = slopes(r, 0, whole, 0, slots)
        terms[r] = own
        terms[r, pl.ds(odd_slot, slots - 1)] = terms[r, pl.ds(odd_slot, slots - 1)] + other
        to_far[r] = terms[r, 2].astype(jnp.bfloat16)
        send(four_down, to_far.at[r], from_far.at[r],
             rev_send.at[0, r], rev_recv.at[0, r], band, col - 2)
        to_partner[r] = pull(other_slope, block).astype(jnp.bfloat16)
        send(True, to_partner.at[r], from_partner.at[r],
             left_send.at[1, r], left_recv.at[1, r], band, partner)
        left_sum[r] = pull(own_slope, whole)

    def return_near(r):
        @pl.when(both(two_down, two_up))
        def _():
            arrive(True, from_far.at[r], rev_send.at[0, r], rev_recv.at[0, r])
            terms[r, 1] = terms[r, 1] + from_far[r].astype(jnp.float32)

        to_near[r] = terms[r, 1].astype(jnp.bfloat16)
        send(two_down, to_near.at[r], from_near.at[r],
             rev_send.at[1, r], rev_recv.at[1, r], band, col - 2)

    def settle_left(r):
        arrive(True, from_partner.at[r], left_send.at[1, r], left_recv.at[1, r])
        total = left_sum[r] + from_partner[r].astype(jnp.float32)
        grad[0, r + 1, pl.ds(EDGE, columns)] = total.astype(jnp.bfloat16)

    def settle(r):
        @pl.when(two_up)
        def _():
            arrive(True, from_near.at[r], rev_send.at[1, r], rev_recv.at[1, r])
            terms[r, 0] = terms[r, 0] + from_near[r].astype(jnp.float32)

        grad[1, r + 1, pl.ds(EDGE, columns)] = terms[r, 0].astype(jnp.bfloat16)

    def grads_out(which):
        halo_out(
            lambda row, rows, first, count: grad.at[which, pl.ds(1 + row, rows), pl.ds(EDGE + first, count)],
            grad, 2 + which,
        )

    stages = ((pass_near, 0), (correlate, 1), (return_near, 3))
    for step in range(height + 3):
        for stage, lag in stages:
            if 0 <= step - lag < height:
                stage(step - lag)
        if step == height:
            for r in range(height):
                settle_left(r)
            grads_out(0)
    for r in range(height):
        settle(r)
    grads_out(1)
    halo_in(grad, 2)
    results[0] = convolve(grad, 0, True).astype(jnp.bfloat16)
    out_left = pltpu.make_async_copy(results.at[0], gl_ref, local_sem.at[5])
    out_left.start()
    halo_in(grad, 3)
    results[1] = convolve(grad, 1, True).astype(jnp.bfloat16)
    out_right = pltpu.make_async_copy(results.at[1], gr_ref, local_sem.at[6])
    out_right.start()
    for cond, describe in pending:
        guarded(cond, lambda: describe().wait_send())
    out_left.wait()
    out_right.wait()


def hand_out(left_ref, right_ref, gl_ref, gr_ref):
    gl_ref[...] = left_ref[...]
    gr_ref[...] = right_ref[...]


def solution(mesh):
    bands, cols = mesh.shape["band"], mesh.shape["col"]

    def shards(left_image, right_image, weights, valid_mask, disparity):
        height, columns, channels = left_image.shape
        slots = DISP // columns // 2 + 1
        wide = columns + 2 * EDGE
        bf16 = jnp.bfloat16
        vmem_spec = pl.BlockSpec(memory_space=pltpu.VMEM)
        any_spec = pl.BlockSpec(memory_space=pl.ANY)
        dma = pltpu.SemaphoreType.DMA
        pad = pltpu.VMEM((2, height + 2, wide, channels), bf16)
        rows = pltpu.VMEM((height, columns, channels), bf16)
        both_rows = pltpu.VMEM((2, height, columns, channels), bf16)
        pixels = pltpu.VMEM((2, height, columns), jnp.int32)

        def body(*refs):
            kernel(bands, cols, *refs)

        grad_left, grad_right = pl.pallas_call(
            body,
            out_shape=(
                jax.ShapeDtypeStruct(left_image.shape, bf16),
                jax.ShapeDtypeStruct(right_image.shape, bf16),
            ),
            in_specs=[any_spec] * 5,
            out_specs=(any_spec, any_spec),
            scratch_shapes=[
                pad,
                pltpu.VMEM(weights.shape, bf16),
                pltpu.VMEM(weights.shape, bf16),
                pixels, pixels,
                pltpu.VMEM((height, slots, columns, channels), bf16),
                both_rows,
                pltpu.VMEM((height, columns, channels), jnp.float32),
                pad,
                pltpu.VMEM((height, slots, columns, channels), jnp.float32),
                both_rows,
                rows, rows, rows,
                rows, rows, rows,
                dma((7,)),
                dma((4, 8)), dma((4, 8)),
                dma((2, height)), dma((2, height)),
                dma((2, height)), dma((2, height)),
                dma((2, height)), dma((2, height)),
                dma((2,)), dma((2,)),
            ],
            compiler_params=pltpu.CompilerParams(
                collective_id=0, has_side_effects=True, vmem_limit_bytes=60 * 2**20
            ),
            cost_estimate=pl.CostEstimate(
                flops=5_000_000_000, bytes_accessed=4_000_000, transcendentals=400_000
            ),
        )(left_image, right_image, weights, valid_mask, disparity)
        return pl.pallas_call(
            hand_out,
            out_shape=(
                jax.ShapeDtypeStruct(left_image.shape, bf16),
                jax.ShapeDtypeStruct(right_image.shape, bf16),
            ),
            in_specs=[vmem_spec, vmem_spec],
            out_specs=(vmem_spec, vmem_spec),
            compiler_params=pltpu.CompilerParams(vmem_limit_bytes=60 * 2**20),
        )(grad_left, grad_right)

    return jax.shard_map(
        shards,
        mesh=mesh,
        in_specs=(
            P("band", "col", None),
            P("band", "col", None),
            P(),
            P("band", "col"),
            P("band", "col"),
        ),
        out_specs=(P("band", "col", None), P("band", "col", None)),
        check_vma=False,
    )
```
